32 devices in a mesh: vocab: 4 (over y, core), dp: 4 (over z), teacher: 2 (over x).
Axes of the slice: x: 2, y: 2, z: 4, core: 2. Of those that a mesh axis runs over, the one named last changes fastest.
Arguments:
- hidden_states: bfloat16 [2048, 4096], P('teacher'), may hold values from -300 to 300
- head_weight: bfloat16 [4096, 16384], P(None, ('vocab', 'dp')), may hold values from -3 to 3
- teacher_logits: bfloat16 [2048, 16384], P(None, ('vocab', 'dp', 'teacher')), may hold values from -20 to 460
- token_weight: float32 [2048], P('teacher'), may hold values from 2 to 20
Outputs:
- hidden_grad: bfloat16 [2048, 4096], P('teacher', ('vocab', 'dp'))
- weight_grad: bfloat16 [4096, 16384], P('teacher', ('vocab', 'dp'))
The draws below stay inside these ranges and needn't reach their ends.
All inputs are finite; a program needn't handle non-finite values.
Results may differ from the reference program's by a relative error of at most 0.005.
Values may be sent and summed in bfloat16 or wider, within the bound.
A program may use at most 192 MiB of HBM per device.

```python
import math
import jax
import jax.numpy as jnp

D = 4096
TOKENS = 2048
V = 16384


def shared_weight(key):
    return jax.random.normal(jax.random.fold_in(key, 101), (D, V), jnp.float32) * (3.0 / math.sqrt(D))


def draw_head_weight(key, part):
    return shared_weight(key).astype(jnp.bfloat16)


def draw_hidden_states(key, part):
    states = jax.random.normal(jax.random.fold_in(key, 202), (TOKENS, D), jnp.float32)
    return states.astype(jnp.bfloat16)


def draw_teacher_logits(key, part):
    values = jax.random.normal(jax.random.fold_in(key, 404), (TOKENS, V), jnp.float32) * 3.0
    return values.astype(jnp.bfloat16)


def block_levels(rng, shape, pieces, smallest, high):
    factor_of = 1.0
    for dim, shards_of in pieces:
        steps = jax.random.uniform(jax.random.fold_in(jax.random.fold_in(rng, 6), dim), (shards_of,), jnp.float32, smallest / len(pieces), high / len(pieces))
        factor_of = factor_of * jnp.repeat(jnp.exp(steps), shape[dim] // shards_of).reshape((-1,) + (1,) * (len(shape) - 1 - dim))
    return factor_of


def setup_inputs(seed: int = 0) -> dict:
    key_of = jax.random.split(jax.random.key(seed), 5)
    hidden_states = draw_hidden_states(jax.random.fold_in(key_of[4], 71), 0)
    head_weight = draw_head_weight(jax.random.fold_in(key_of[4], 71), 0)
    teacher_logits = draw_teacher_logits(jax.random.fold_in(key_of[4], 71), 0)
    token_weight = jnp.clip(jnp.exp(math.log(20.0) - 2.3025851 * jax.random.uniform(key_of[3], (TOKENS,), jnp.float32) ** block_levels(key_of[3], (TOKENS,), ((0, 2),), -0.2, 0.2)), 2.0, 20.0)
    return {"hidden_states": hidden_states, "head_weight": head_weight, "teacher_logits": teacher_logits, "token_weight": token_weight}


def row_norm(values):
    top_value = jnp.max(values, axis=1, keepdims=True)
    return top_value + jnp.log(jnp.sum(jnp.exp(values - top_value), axis=1, keepdims=True))


def reference(hidden_states, head_weight, teacher_logits, token_weight):
    logits = jnp.dot(hidden_states, head_weight, preferred_element_type=jnp.float32)
    student_norm = row_norm(logits)
    teacher = teacher_logits.astype(jnp.float32)
    teacher_norm = row_norm(teacher)
    logit_grad = (token_weight[:, None] * (jnp.exp(logits - student_norm) - jnp.exp(teacher - teacher_norm))).astype(jnp.bfloat16)
    hidden_grad = jnp.dot(logit_grad, head_weight.T, preferred_element_type=jnp.float32).astype(jnp.bfloat16)
    weight_grad = jnp.dot(hidden_states.T, logit_grad, preferred_element_type=jnp.float32).astype(jnp.bfloat16)
    return hidden_grad, weight_grad
```

```python
import functools

import jax
import jax.numpy as jnp
from jax import lax
from jax.experimental import pallas as pl
from jax.experimental.pallas import tpu as pltpu
from jax.sharding import PartitionSpec as P

MESH = pl.DeviceIdType.MESH
F32 = jnp.float32
BF16 = jnp.bfloat16
LANES = 128
CHUNKS = 4
ROWS = 32


def flip(v, mask):
    out = v
    bit = 1
    while bit <= mask:
        if mask & bit:
            out = out + bit * (1 - 2 * ((v // bit) % 2))
        bit *= 2
    return out


def low_bit(m):
    return m & (-m)


def aligned(start, size):
    return pl.ds(pl.multiple_of(start, size), size)


def kernel(nv, nd, nt, h_hbm, w_hbm, t_hbm, tw_ref, hid_ref, wg_hbm,
           W, H, Ho, S, T, G, Go, sb, rb, zs, zr, WA, stage, ST, stats,
           w_sem, h_sem, tl_sem, out_sem,
           tx_s, tx_r, hx_s, hx_r, hz_s, hz_r, hv_s, hv_r,
           st_s, st_r, gx_s, gx_r, rs_s, rs_r, z_s, z_r):
    v = lax.axis_index("vocab")
    d = lax.axis_index("dp")
    t = lax.axis_index("teacher")
    plane = nv * nd
    me = v * nd + d
    tok, D = H.shape
    vs = W.shape[1]
    vt = T.shape[2]
    dh = D // nt
    R = tok // plane
    dv = D // nv
    dz = dv // nd
    tc = tok // CHUNKS

    def plane_peer(k):
        p = (me + k) % plane
        return (p // nd, p % nd, t)

    def t_peer(k):
        return (v, d, (t + k) % nt)

    bar = pltpu.get_barrier_semaphore()
    for k in range(1, plane):
        pl.semaphore_signal(bar, inc=1, device_id=plane_peer(k), device_id_type=MESH)
    for k in range(1, nt):
        pl.semaphore_signal(bar, inc=1, device_id=t_peer(k), device_id_type=MESH)

    wn = w_sem.shape[0]
    hn = h_sem.shape[0]
    wc = vs // wn
    hc = tok // hn
    w_cp = [pltpu.make_async_copy(w_hbm.at[:, pl.ds(i * wc, wc)], W.at[:, pl.ds(i * wc, wc)], w_sem.at[i]) for i in range(wn)]
    h_cp = [pltpu.make_async_copy(h_hbm.at[pl.ds(i * hc, hc)], H.at[pl.ds(i * hc, hc)], h_sem.at[i]) for i in range(hn)]
    h_cp[0].start()
    w_cp[0].start()
    for i in range(1, wn):
        w_cp[i].start()
    for i in range(1, hn):
        h_cp[i].start()
    tl_cp = pltpu.make_async_copy(t_hbm.at[aligned(t * tok, tok)], T.at[t], tl_sem)
    tl_cp.start()
    pl.semaphore_wait(bar, plane + nt - 2)

    def remote(src, dst, ss, rs, dev):
        return pltpu.make_async_remote_copy(src_ref=src, dst_ref=dst, send_sem=ss, recv_sem=rs, device_id=dev, device_id_type=MESH)

    sent = []
    hx = []
    for k in range(1, nt):
        p = (t + k) % nt
        hx.append(remote(h_hbm.at[aligned(me * R, R), aligned(p * dh, dh)], Ho.at[k - 1, aligned(me * R, R)],
                         hx_s.at[k - 1], hx_r.at[k - 1], t_peer(k)))
        hx[-1].start()
    tx = []
    for k in range(1, nt):
        p = (t + k) % nt
        tx.append(remote(t_hbm.at[aligned(p * tok, tok)], T.at[t], tx_s.at[k - 1], tx_r.at[k - 1], t_peer(k)))
        tx[-1].start()
    sent += hx + tx

    def logits(i, j):
        def body(n, _):
            c = aligned(j * wc + n * 256, 256) if wc > 256 else pl.ds(j * wc, wc)
            S[pl.ds(i * hc, hc), c] = jnp.dot(H[pl.ds(i * hc, hc), :], W[:, c], preferred_element_type=F32)
            return 0
        lax.fori_loop(0, max(wc // 256, 1), body, 0)

    hz = []
    hv = []
    order = []
    bit = nv // 2
    held = [0]
    n = 0
    while bit >= 1:
        order.append((bit, [(m, n + i) for i, m in enumerate(held)]))
        n += len(held)
        held = held + [m + bit for m in held]
        bit //= 2

    def start_hz():
        for c in hx:
            c.wait_recv()
        for b in range(nt - 1):
            for k in range(1, nd):
                rows = aligned(me * R, R)
                i = b * (nd - 1) + k - 1
                hz.append(remote(Ho.at[b, rows], Ho.at[b, rows], hz_s.at[i], hz_r.at[i], (v, (d + k) % nd, t)))
                hz[-1].start()

    def start_hv(stage_i):
        bit, items = order[stage_i]
        out = []
        for b in range(nt - 1):
            for m, i in items:
                rows = aligned(flip(v, m) * (nd * R), nd * R)
                i = b * (nv - 1) + i
                out.append(remote(Ho.at[b, rows], Ho.at[b, rows], hv_s.at[i], hv_r.at[i], (flip(v, bit), d, t)))
                out[-1].start()
        hv.append(out)

    for i in range(hn):
        h_cp[i].wait()
        for j in range(wn):
            if i == 0:
                w_cp[j].wait()
            logits(i, j)
        if i == 0:
            start_hz()

    lane = lax.broadcasted_iota(jnp.int32, (ROWS, LANES), 1)

    def s_stats(n, _):
        r = aligned(n * ROWS, ROWS)
        s = S[r, :]
        m = jnp.max(s, axis=1, keepdims=True)
        e = jnp.exp(s - m)
        S[r, :] = e
        ST[r, :] = jnp.where(lane == 0, m, jnp.sum(e, axis=1, keepdims=True))
        return 0

    lax.fori_loop(0, tok // ROWS, s_stats, 0)

    tl_cp.wait()
    for c in tx:
        c.wait_recv()

    def t_stats(n, _):
        r = aligned(n * ROWS, ROWS)
        parts = [T[j, r, :].astype(F32) for j in range(nt)]
        m = functools.reduce(jnp.maximum, [jnp.max(x, axis=1, keepdims=True) for x in parts])
        l = functools.reduce(jnp.add, [jnp.sum(jnp.exp(x - m), axis=1, keepdims=True) for x in parts])
        ST[r, :] = jnp.where(lane < 2, ST[r, :], jnp.where(lane == 2, m, l))
        return 0

    lax.fori_loop(0, tok // ROWS, t_stats, 0)

    for j in range(tok // LANES):
        c = pl.ds(j * LANES, LANES)
        stats[0, :, c] = ST[c, :].T[0:8, :]

    st = []
    for k in range(1, plane):
        st.append(remote(stats.at[0], stats.at[k], st_s.at[k - 1], st_r.at[k - 1], plane_peer(k)))
        st[-1].start()
    sent += st

    for c in hz:
        c.wait_recv()
    start_hv(0)

    for c in st:
        c.wait_recv()

    tops = jnp.max(stats[...], axis=0)
    s_top = tops[0:1]
    t_top = tops[2:3]
    s_sum = jnp.sum(stats[:, 1, :] * jnp.exp(stats[:, 0, :] - s_top), axis=0, keepdims=True)
    t_sum = jnp.sum(stats[:, 3, :] * jnp.exp(stats[:, 2, :] - t_top), axis=0, keepdims=True)
    s_norm = s_top + jnp.log(s_sum)
    t_norm = t_top + jnp.log(t_sum)
    tw = tw_ref[...]
    fac = tw * jnp.exp(stats[0, 0:1, :] - s_norm)
    row = lax.broadcasted_iota(jnp.int32, (LANES, tok), 0)
    mat = jnp.where(row == 0, fac, jnp.where(row == 1, t_norm, tw))
    for j in range(tok // LANES):
        ST[j * LANES:(j + 1) * LANES, :] = mat[:, j * LANES:(j + 1) * LANES].T

    def make_grad(c):
        def body(n, _):
            r = aligned(c * tc + n * ROWS, ROWS)
            a = ST[r, 0:1]
            tn = ST[r, 1:2]
            w = ST[r, 2:3]
            for j in range(nt):
                cols = pl.ds(j * vt, vt)
                G[r, cols] = (S[r, cols] * a - w * jnp.exp(T[j, r, :].astype(F32) - tn)).astype(BF16)
            return 0
        lax.fori_loop(0, tc // ROWS, body, 0)

    gx = [[] for _ in range(CHUNKS)]

    def send_grad(c):
        r = pl.ds(c * tc, tc)
        for k in range(1, nt):
            i = (k - 1) * CHUNKS + c
            cp = remote(G.at[r], Go.at[k - 1, r], gx_s.at[i], gx_r.at[i], t_peer(k))
            cp.start()
            gx[c].append(cp)
            sent.append(cp)

    DT = min(dv, 512)

    def share(c, m, dst, adds):
        base = flip(v, m) * dv

        def body(n, _):
            r = aligned(n * DT, DT)
            p = lax.dot_general(W[aligned(base + n * DT, DT), :], G[pl.ds(c * tc, tc), :],
                                (((1,), (1,)), ((), ())), preferred_element_type=F32)
            for s in adds:
                p = p + rb[s - 1, c, r, :].astype(F32)
            dst[r, :] = p.astype(BF16)
            return 0
        lax.fori_loop(0, dv // DT, body, 0)

    rs = {}

    def send_share(c, m):
        low = low_bit(m)
        adds = []
        b = 1
        while b < low:
            adds.append(m ^ b)
            b *= 2
        for s in adds:
            rs[(c, s)].wait_recv()
        share(c, m, sb.at[m - 1, c], adds)
        i = (m - 1) * CHUNKS + c
        cp = remote(sb.at[m - 1, c], rb.at[m - 1, c], rs_s.at[i], rs_r.at[i], (flip(v, low), d, t))
        cp.start()
        rs[(c, m)] = cp
        sent.append(cp)

    first = [m for m in range(nv - 1, 0, -1) if low_bit(m) == 1]
    later = sorted([m for m in range(1, nv) if low_bit(m) > 1], key=lambda m: (low_bit(m), -m))

    zc = [[] for _ in range(CHUNKS)]

    def to_dp(c):
        adds = []
        b = 1
        while b < nv:
            adds.append(b)
            b *= 2
        for s in adds:
            rs[(c, s)].wait_recv()
        share(c, 0, zs.at[c], adds)
        for k in range(1, nd):
            i = (k - 1) * CHUNKS + c
            p = (d + k) % nd
            cp = remote(zs.at[c, aligned(p * dz, dz)], zr.at[k - 1, c], z_s.at[i], z_r.at[i], (v, p, t))
            cp.start()
            zc[c].append(cp)
            sent.append(cp)

    def finish(c):
        for cp in zc[c]:
            cp.wait_recv()
        x = zs[c, aligned(d * dz, dz), :].astype(F32)
        for k in range(1, nd):
            x = x + zr[k - 1, c].astype(F32)
        hid_ref[:, c * tc:(c + 1) * tc] = x.astype(BF16)

    wt = 256
    n_w = dh // wt

    def own_weight(i0, i1):
        def body(i, _):
            WA[aligned(i * wt, wt), :] = lax.dot_general(
                H[:, aligned(t * dh + i * wt, wt)], G[...], (((0,), (0,)), ((), ())), preferred_element_type=F32)
            return 0
        lax.fori_loop(i0, i1, body, 0)

    def part_a(c):
        make_grad(c)
        send_grad(c)
        for m in first:
            send_share(c, m)

    def part_b(c):
        for m in later:
            send_share(c, m)

    part_a(0)
    for c in range(1, CHUNKS):
        part_a(c)
        part_b(c - 1)
    part_b(CHUNKS - 1)
    sent += hz
    for c in hv[0]:
        c.wait_recv()
    for s in range(1, len(order)):
        start_hv(s)
        if s < len(order) - 1:
            for c in hv[s]:
                c.wait_recv()
    for c in range(CHUNKS):
        own_weight(c * n_w // CHUNKS, (c + 1) * n_w // CHUNKS)
        to_dp(c)
    for out in hv[1:][-1:]:
        for c in out:
            c.wait_recv()
    for out in hv:
        sent += out
    for c in range(CHUNKS):
        for cp in gx[c]:
            cp.wait_recv()

    def out_copy(i, slot):
        return pltpu.make_async_copy(stage.at[slot], wg_hbm.at[aligned(i * wt, wt)], out_sem.at[slot])

    def last_weight(i, _):
        slot = i % 2

        @pl.when(i >= 2)
        def _():
            out_copy(i - 2, slot).wait()
        x = WA[aligned(i * wt, wt), :]
        for b in range(nt - 1):
            x = x + lax.dot_general(Ho[b, :, aligned(i * wt, wt)], Go[b], (((0,), (0,)), ((), ())), preferred_element_type=F32)
        stage[slot] = x.astype(BF16)
        out_copy(i, slot).start()
        return 0

    lax.fori_loop(0, n_w, last_weight, 0)
    for c in range(CHUNKS):
        finish(c)
    for i in range(n_w - 2, n_w):
        out_copy(i, i % 2).wait()
    for cp in sent:
        cp.wait_send()


def per_device(nv, nd, nt, hidden_states, head_weight, teacher_logits, token_weight):
    tok, D = hidden_states.shape
    vs = head_weight.shape[1]
    vt = teacher_logits.shape[1]
    plane = nv * nd
    dv = D // nv
    dz = dv // nd
    dh = D // nt
    tc = tok // CHUNKS
    dma = lambda n: pltpu.SemaphoreType.DMA((n,))
    scratch = [
        pltpu.VMEM((D, vs), BF16),
        pltpu.VMEM((tok, D), BF16),
        pltpu.VMEM((nt - 1, tok, dh), BF16),
        pltpu.VMEM((tok, vs), F32),
        pltpu.VMEM((nt, tok, vt), BF16),
        pltpu.VMEM((tok, vs), BF16),
        pltpu.VMEM((nt - 1, tok, vs), BF16),
        pltpu.VMEM((nv - 1, CHUNKS, dv, tc), BF16),
        pltpu.VMEM((nv - 1, CHUNKS, dv, tc), BF16),
        pltpu.VMEM((CHUNKS, dv, tc), BF16),
        pltpu.VMEM((nd - 1, CHUNKS, dz, tc), BF16),
        pltpu.VMEM((dh, vs), F32),
        pltpu.VMEM((2, 256, vs), BF16),
        pltpu.VMEM((tok, LANES), F32),
        pltpu.VMEM((plane, 8, tok), F32),
        dma(4), dma(2), pltpu.SemaphoreType.DMA, dma(2),
        dma(nt - 1), dma(nt - 1), dma(nt - 1), dma(nt - 1),
        dma((nt - 1) * (nd - 1)), dma((nt - 1) * (nd - 1)),
        dma((nt - 1) * (nv - 1)), dma((nt - 1) * (nv - 1)),
        dma(plane - 1), dma(plane - 1),
        dma((nt - 1) * CHUNKS), dma((nt - 1) * CHUNKS),
        dma((nv - 1) * CHUNKS), dma((nv - 1) * CHUNKS),
        dma((nd - 1) * CHUNKS), dma((nd - 1) * CHUNKS),
    ]
    any_spec = pl.BlockSpec(memory_space=pl.ANY)
    vmem_spec = pl.BlockSpec(memory_space=pltpu.VMEM)
    hid, wg = pl.pallas_call(
        functools.partial(kernel, nv, nd, nt),
        out_shape=(jax.ShapeDtypeStruct((dz, tok), BF16), jax.ShapeDtypeStruct((dh, vs), BF16)),
        in_specs=[any_spec, any_spec, any_spec, vmem_spec],
        out_specs=(vmem_spec, any_spec),
        scratch_shapes=scratch,
        compiler_params=pltpu.CompilerParams(
            collective_id=0, has_side_effects=True, vmem_limit_bytes=62 * 1024 * 1024),
    )(hidden_states, head_weight, teacher_logits, token_weight.reshape(1, tok))
    return hid.T, wg


def solution(mesh):
    sizes = mesh.shape
    return jax.shard_map(
        functools.partial(per_device, sizes["vocab"], sizes["dp"], sizes["teacher"]),
        mesh=mesh,
        in_specs=(
            P("teacher", None),
            P(None, ("vocab", "dp")),
            P(None, ("vocab", "dp", "teacher")),
            P("teacher"),
        ),
        out_specs=(P("teacher", ("vocab", "dp")), P("teacher", ("vocab", "dp"))),
        check_vma=False,
    )
```
